512 devices in a mesh: tok: 128 (over z, x, core), grp: 4 (over y).
Axes of the slice: x: 4, y: 4, z: 16, core: 2. Of those that a mesh axis runs over, the one named last changes fastest.
Arguments:
- queries: bfloat16 [24576, 2048], P('tok', 'grp'), may hold values from -72 to 72
- new_keys: bfloat16 [24576, 2048], P('tok', 'grp'), may hold values from -8 to 8
- new_values: bfloat16 [24576, 2048], P('tok', 'grp'), may hold values from -6 to 6
- residual: bfloat16 [24576, 2048], P('tok', 'grp'), may hold values from -6 to 6
- w_out: bfloat16 [2048, 2048], P('grp'), may hold values from -0.125 to 0.125
- leaf_keys: bfloat16 [128, 512, 2048], P('tok', None, 'grp'), may hold values from -6 to 6
- leaf_values: bfloat16 [128, 512, 2048], P('tok', None, 'grp'), may hold values from -6 to 6
- upper_keys: bfloat16 [6, 1024, 2048], P(None, 'tok', 'grp'), may hold values from -8 to 8
- upper_values: bfloat16 [6, 1024, 2048], P(None, 'tok', 'grp'), may hold values from -6 to 6
- req_len: int32 [128], replicated, may hold values from 48 to 192, as said below
- leaf_mid: int32 [128], replicated, may hold values from 0 to 3
- mid_root: int32 [4], replicated, may hold values from 0 to 1, as said below
- upper_len: int32 [6], replicated, may hold values from 256 to 1024, as said below
- leaf_len: int32 [128], replicated, may hold values from 128 to 512, as said below
Outputs:
- hidden_out: bfloat16 [24576, 2048], P('tok', 'grp')
The draws below stay inside these ranges and needn't reach their ends.
Inputs may be any that keep to these rules, and one draw needn't show every extreme that they name: `req_len`: some request has exactly 192 new tokens. `mid_root`: each root is the parent of 2 mids. `upper_len`: the first 2 entries are roots and equal 1024. `leaf_len`: some leaf has exactly 512 positions.
All inputs are finite; a program needn't handle non-finite values.
Results may differ from the reference program's by a relative error of at most 0.008.
Values may be sent and summed in bfloat16 or wider, within the bound.
A program may use at most 64 MiB of HBM per device.

```python
import math
import jax
import jax.numpy as jnp
from jax import lax

D = 2048
HEADS = 16
HEAD_DIM = 128
HD = 2048
TOK_DEV = 192
LEAF_POS = 512
UPPER_LEN = 1024
ROOTS = 2
MIDS = 4
UPPERS = 6
REQS = 128
TOKENS = 24576


def draw_queries(key, part):
    sample = jnp.clip(3.0 * jax.random.normal(jax.random.fold_in(key, 7002), (TOKENS, HD), jnp.float32), -18.0, 18.0)
    return sample.astype(jnp.bfloat16)


def draw_new_keys(key, part):
    sample = jnp.clip(jax.random.normal(jax.random.fold_in(key, 7005), (TOKENS, HD), jnp.float32), -6.0, 6.0)
    return sample.astype(jnp.bfloat16)


def draw_upper_keys(key, part):
    sample = jnp.clip(jax.random.normal(jax.random.fold_in(key, 7030), (UPPERS, UPPER_LEN, HD), jnp.float32), -6.0, 6.0)
    return sample.astype(jnp.bfloat16)


def draw_req_len(key, part):
    drawn = jax.random.randint(jax.random.fold_in(key, 7020), (REQS,), TOK_DEV // 4, TOK_DEV + 1)
    chosen = jax.random.randint(jax.random.fold_in(key, 7021), (), 0, REQS)
    return jnp.where(jnp.arange(REQS) == chosen, TOK_DEV, drawn).astype(jnp.int32)


def draw_mid_root(key, part):
    return (jax.random.permutation(jax.random.fold_in(key, 7010), MIDS) % ROOTS).astype(jnp.int32)


def draw_upper_len(key, part):
    mids_len = jax.random.randint(jax.random.fold_in(key, 7011), (MIDS,), UPPER_LEN // 4, UPPER_LEN + 1)
    return jnp.concatenate([jnp.full((ROOTS,), UPPER_LEN, jnp.int32), mids_len.astype(jnp.int32)])


def draw_leaf_len(key, part):
    lengths_drawn = jax.random.randint(jax.random.fold_in(key, 7012), (REQS,), LEAF_POS // 4, LEAF_POS + 1)
    chosen = jax.random.randint(jax.random.fold_in(key, 7013), (), 0, REQS)
    return jnp.where(jnp.arange(REQS) == chosen, LEAF_POS, lengths_drawn).astype(jnp.int32)


def with_ends(values, rng, smallest, top_value):
    longest = values.shape.index(max(values.shape))
    spots = []
    for shift in (0, 1):
        where = [jax.random.randint(jax.random.fold_in(rng, axis), (), 0, length) for axis, length in enumerate(values.shape)]
        where[longest] = (where[longest] + shift) % values.shape[longest]
        spots.append(tuple(where))
    return values.at[spots[0]].set(smallest).at[spots[1]].set(top_value)


def block_scale(rng, extent, cuts, low, largest):
    loudness, own = 1.0, jax.random.fold_in(rng, 6)
    for position, shards_of in cuts:
        steps = jnp.exp(jax.random.uniform(jax.random.fold_in(own, position), (shards_of,), jnp.float32, low / len(cuts), largest / len(cuts)))
        loudness = loudness * jnp.repeat(steps, extent[position] // shards_of).reshape([-1 if axis == position else 1 for axis in range(len(extent))])
    return loudness


def bell_draw(own_key, extent, scale, most, cuts=(), kind=jnp.bfloat16):
    result = scale * jax.random.normal(own_key, extent, jnp.float32)
    if cuts:
        result = result * block_scale(own_key, extent, cuts, -0.22, 0.18)
    return jnp.clip(result, -most, most).astype(kind)


def setup_inputs(seed: int = 0) -> dict:
    key_list = jax.random.split(jax.random.key(seed), 15)
    return {
        "queries": draw_queries(jax.random.fold_in(key_list[14], 71), 0),
        "new_keys": draw_new_keys(jax.random.fold_in(key_list[14], 71), 0),
        "new_values": bell_draw(key_list[2], (TOKENS, HD), 1.0, 6.0, ((0, 128), (1, 4))),
        "residual": bell_draw(key_list[3], (TOKENS, D), 1.0, 6.0, ((0, 128), (1, 4))),
        "w_out": bell_draw(key_list[4], (HD, D), HD ** -0.5, 0.125, ((0, 4),)),
        "leaf_keys": bell_draw(key_list[5], (REQS, LEAF_POS, HD), 1.0, 6.0, ((0, 128), (2, 4))),
        "leaf_values": bell_draw(key_list[6], (REQS, LEAF_POS, HD), 1.0, 6.0, ((0, 128), (2, 4))),
        "upper_keys": draw_upper_keys(jax.random.fold_in(key_list[14], 71), 0),
        "upper_values": bell_draw(key_list[8], (UPPERS, UPPER_LEN, HD), 1.0, 6.0, ((1, 128), (2, 4))),
        "req_len": draw_req_len(jax.random.fold_in(key_list[14], 71), 0),
        "leaf_mid": with_ends(jax.random.randint(key_list[10], (REQS,), 0, MIDS), jax.random.fold_in(key_list[10], 1), 0, MIDS - 1).astype(jnp.int32),
        "mid_root": draw_mid_root(jax.random.fold_in(key_list[14], 71), 0),
        "upper_len": draw_upper_len(jax.random.fold_in(key_list[14], 71), 0),
        "leaf_len": draw_leaf_len(jax.random.fold_in(key_list[14], 71), 0),
    }


NEG_FILL = -1e+30

def heads_of(matrix):
    return matrix.astype(jnp.float32).reshape(matrix.shape[0], HEADS, HEAD_DIM)

def reference(queries, new_keys, new_values, residual, w_out, leaf_keys, leaf_values, upper_keys, upper_values, req_len, leaf_mid, mid_root, upper_len, leaf_len):
    score_scale = 1.0 / math.sqrt(HEAD_DIM)
    offsets = jnp.arange(TOK_DEV, dtype=jnp.int32)
    upper_pos = jnp.arange(UPPER_LEN, dtype=jnp.int32)
    leaf_pos = jnp.arange(LEAF_POS, dtype=jnp.int32)

    def one_request(request):
        is_valid = offsets < req_len[request]
        row_index = (request * TOK_DEV + offsets).astype(jnp.int32)
        mid_node = leaf_mid[request].astype(jnp.int32)
        root_node = mid_root[mid_node].astype(jnp.int32)
        mid_index = (ROOTS + mid_node).astype(jnp.int32)
        key_rows = jnp.concatenate([upper_keys[root_node], upper_keys[mid_index], leaf_keys[request], new_keys[row_index]], axis=0)
        value_rows = jnp.concatenate([upper_values[root_node], upper_values[mid_index], leaf_values[request], new_values[row_index]], axis=0)
        fixed_allowed = jnp.concatenate([upper_pos < upper_len[root_node], upper_pos < upper_len[mid_index], leaf_pos < leaf_len[request]])
        new_allowed = (offsets[None, :] <= offsets[:, None]) & is_valid[None, :]
        allowed = jnp.concatenate([jnp.broadcast_to(fixed_allowed[None, :], (TOK_DEV, fixed_allowed.shape[0])), new_allowed], axis=1)
        scores = jnp.einsum('qhd,khd->hqk', heads_of(queries[row_index]), heads_of(key_rows)) * score_scale
        scores = jnp.where(allowed[None], scores, NEG_FILL)
        row_max = lax.optimization_barrier(jnp.max(scores, axis=2, keepdims=True))
        exp_scores = jnp.where(allowed[None], jnp.exp(scores - row_max), 0.0)
        row_total = lax.optimization_barrier(jnp.sum(exp_scores, axis=2))
        weights = lax.optimization_barrier(exp_scores.astype(jnp.bfloat16)).astype(jnp.float32)
        weighted = jnp.einsum('hqk,khd->hqd', weights, heads_of(value_rows))
        attended = (weighted / row_total[:, :, None]).transpose(1, 0, 2).reshape(TOK_DEV, HEADS * HEAD_DIM)
        return jnp.where(is_valid[:, None], attended, 0.0).astype(jnp.bfloat16)
    attended = lax.map(one_request, jnp.arange(REQS, dtype=jnp.int32))
    attention = attended.reshape(TOKENS, HEADS * HEAD_DIM)
    projected = jnp.dot(attention, w_out, preferred_element_type=jnp.float32)
    return (residual.astype(jnp.float32) + projected).astype(jnp.bfloat16)
```

```python
import functools

import jax
import jax.numpy as jnp
from jax import lax
from jax.experimental import pallas as pl
from jax.experimental.pallas import tpu as pltpu
from jax.sharding import PartitionSpec as P

HEAD_DIM = 128
NEG_FILL = -1e30
LOG2E = 1.4426950408889634
CHIPS_X = 4
CORES = 2
MESH = pl.DeviceIdType.MESH


def dot_nt(a, b):
    return lax.dot_general(a, b, (((1,), (1,)), ((), ())), preferred_element_type=jnp.float32)


def wait_bytes(view, sem):
    pltpu.make_async_copy(view, view, sem).wait()


def col_to_row(col):
    pieces = []
    for start in range(0, col.shape[0], 128):
        piece = col[start : start + 128]
        n = piece.shape[0]
        diag = lax.broadcasted_iota(jnp.int32, (n, 128), 0) == lax.broadcasted_iota(
            jnp.int32, (n, 128), 1
        )
        spread = jnp.broadcast_to(piece, (n, 128))
        pieces.append(jnp.sum(jnp.where(diag, spread, 0.0), axis=0, keepdims=True))
    return jnp.concatenate(pieces, axis=1)


def row_to_col(row, n_rows):
    pieces = []
    for start in range(0, n_rows, 128):
        n = min(128, n_rows - start)
        diag = lax.broadcasted_iota(jnp.int32, (n, 128), 0) == lax.broadcasted_iota(
            jnp.int32, (n, 128), 1
        )
        spread = jnp.broadcast_to(row[:, start : start + 128], (n, 128))
        pieces.append(jnp.sum(jnp.where(diag, spread, 0.0), axis=1, keepdims=True))
    return jnp.concatenate(pieces, axis=0)


def softmax_part(parts):
    scale = HEAD_DIM ** (-0.5) * LOG2E
    top = functools.reduce(
        jnp.maximum, [jnp.max(s, axis=1, keepdims=True) for s, _ in parts]
    )
    total, weighted = 0.0, 0.0
    for s, v in parts:
        exps = jnp.exp2((s - top) * scale)
        total = total + jnp.sum(exps, axis=1, keepdims=True)
        weighted = weighted + jnp.dot(
            exps.astype(jnp.bfloat16), v, preferred_element_type=jnp.float32
        )
    return weighted / total, top * scale + jnp.log(total) * LOG2E


def kernel(
    nx,
    nz,
    ny,
    heads,
    roots,
    req_len,
    leaf_mid,
    mid_root,
    upper_len,
    leaf_len,
    uk,
    uv,
    q_hbm,
    nk_hbm,
    nv_hbm,
    res_hbm,
    w_hbm,
    lk_hbm,
    lv_hbm,
    out,
    *scratch,
):
    kv = scratch[:heads]
    (
        up,
        up_other,
        qx,
        lk,
        lv,
        nk,
        nv,
        res,
        w,
        leaf_o,
        leaf_lse,
        o_send,
        o_recv,
        s_send,
        s_recv,
        at,
        acc,
        in_sem,
        pre_sem,
        ring_send,
        ring_recv,
        sib_send,
        sib_recv,
        q_sem,
        w_sem,
        wf_sem,
        o_sem_s,
        o_sem_r,
        s_sem_s,
        s_sem_r,
        y_sem_s,
        y_sem_r,
    ) = scratch[heads:]
    nodes = kv[0].shape[2]
    rows = qx.shape[1]
    width = heads * HEAD_DIM
    half_rows = width // CORES
    tok, y = lax.axis_index("tok"), lax.axis_index("grp")
    c = lax.rem(tok, CORES)
    x = lax.rem(lax.div(tok, CORES), nx)
    z = lax.div(tok, CORES * nx)

    def dev(z_, x_, c_, y_):
        return ((z_ * nx + x_) * CORES + c_, y_)

    sibling = dev(z, x, 1 - c, y)
    right = dev(lax.rem(z + 1, nz), x, c, y)
    left = dev(lax.rem(z + nz - 1, nz), x, c, y)

    def x_mate(k):
        return lax.rem(x + k, nx)

    def y_mate(k):
        return lax.rem(y + k, ny)

    loads = [
        (uk, up.at[0]),
        (uv, up.at[1]),
        (q_hbm, qx.at[x]),
        (lk_hbm, lk),
        (lv_hbm, lv),
        (nk_hbm, nk),
        (nv_hbm, nv),
        (res_hbm, res),
        (w_hbm.at[:, pl.ds(pl.multiple_of(y * width, width), width)], w.at[y]),
    ]
    loads = [pltpu.make_async_copy(a, b, in_sem.at[i]) for i, (a, b) in enumerate(loads)]
    for load in loads:
        load.start()

    partners = [sibling, right, left]
    partners += [dev(z, x_mate(k), c, y) for k in range(1, nx)]
    partners += [dev(z, x, c, y_mate(k)) for k in range(1, ny)]
    barrier = pltpu.get_barrier_semaphore()
    for partner in partners:
        pl.semaphore_signal(barrier, inc=1, device_id=partner, device_id_type=MESH)
    pl.semaphore_wait(barrier, len(partners))

    def send(src, dst, send_sem, recv_sem, device):
        pltpu.make_async_remote_copy(
            src_ref=src,
            dst_ref=dst,
            send_sem=send_sem,
            recv_sem=recv_sem,
            device_id=device,
            device_id_type=MESH,
        ).start()

    loads[0].wait()
    loads[1].wait()
    send(up.at[1 - c], up_other, pre_sem.at[0], pre_sem.at[1], sibling)
    for k in range(1, nx):
        send(q_hbm, qx.at[x], q_sem.at[0], q_sem.at[1], dev(z, x_mate(k), c, y))
    my_half = pl.ds(pl.multiple_of(c * half_rows, half_rows), half_rows)
    for k in range(1, ny):
        to = y_mate(k)
        send(
            w_hbm.at[my_half, pl.ds(pl.multiple_of(to * width, width), width)],
            w.at[y, my_half],
            w_sem.at[0],
            w_sem.at[1],
            dev(z, x, c, to),
        )
    wait_bytes(up_other, pre_sem.at[1])
    mine = up[c].astype(jnp.float32).reshape(nodes, 8, width)
    other = up_other[...].astype(jnp.float32).reshape(nodes, 8, width)
    first = jnp.where(c == 0, mine, other)
    second = jnp.where(c == 0, other, mine)
    block = jnp.concatenate([first, second], axis=1).astype(jnp.bfloat16)
    for h in range(heads):
        kv[h][c, z] = block[:, :, h * HEAD_DIM : (h + 1) * HEAD_DIM]

    steps = nz // 2
    cut = nodes // 2

    def ring_view(h, direction, step):
        slot = lax.rem(z + (nz - step if direction == 0 else step), nz)
        view = kv[h].at[c, slot]
        return view

    def ring_part(h, direction, step, hop):
        view = ring_view(h, direction, step)
        if hop == steps:
            view = view.at[pl.ds(0, cut)] if direction == 0 else view.at[pl.ds(cut, nodes - cut)]
        return view

    def ring_start(h, direction, step):
        view = ring_part(h, direction, step, step + 1)
        send(
            view,
            view,
            ring_send.at[h],
            ring_recv.at[h, direction, step],
            right if direction == 0 else left,
        )

    def ring_wait(h, direction, step):
        wait_bytes(
            ring_part(h, direction, step + 1, step + 1), ring_recv.at[h, direction, step]
        )

    def share(h, view):
        send(view, view, sib_send.at[h], sib_recv.at[h], sibling)

    for h in range(heads):
        for direction in range(2):
            ring_start(h, direction, 0)
    for h in range(heads):
        share(h, kv[h].at[c, z])

    me = tok
    position = lax.broadcasted_iota(jnp.int32, (rows, 1), 0)

    def leaf_part(h):
        cols = slice(h * HEAD_DIM, (h + 1) * HEAD_DIM)
        query = qx[x, :, cols]
        leaf_scores = dot_nt(query, lk[:, cols])
        at_pos = lax.broadcasted_iota(jnp.int32, leaf_scores.shape, 1)
        leaf_scores = jnp.where(at_pos < leaf_len[me], leaf_scores, NEG_FILL)
        new_scores = dot_nt(query, nk[:, cols])
        key_pos = lax.broadcasted_iota(jnp.int32, new_scores.shape, 1)
        query_pos = lax.broadcasted_iota(jnp.int32, new_scores.shape, 0)
        allowed = (key_pos <= query_pos) & (key_pos < req_len[me])
        new_scores = jnp.where(allowed, new_scores, NEG_FILL)
        o, lse = softmax_part([(leaf_scores, lv[:, cols]), (new_scores, nv[:, cols])])
        leaf_o[h] = o
        leaf_lse[h] = jnp.broadcast_to(lse, (rows, HEAD_DIM))

    for step in range(steps - 1):
        for h in range(heads):
            for direction in range(2):
                ring_wait(h, direction, step)
                ring_start(h, direction, step + 1)
                share(h, ring_view(h, direction, step + 1))
        if step == 0:
            for load in loads[2:7]:
                load.wait()
            for h in range(max(0, heads - steps + 1)):
                leaf_part(h)
        h = step + max(0, heads - steps + 1)
        if h < heads:
            leaf_part(h)
    for h in range(heads):
        for direction in range(2):
            ring_wait(h, direction, steps - 1)
        share(h, ring_view(h, 0, steps))

    wait_bytes(w.at[pl.ds(0, ny - 1), pl.ds(0, half_rows)], w_sem.at[1])
    for k in range(1, ny):
        view = w.at[y_mate(k), my_half]
        send(view, view, wf_sem.at[0], wf_sem.at[1], sibling)
    wait_bytes(qx.at[pl.ds(0, nx - 1)], q_sem.at[1])

    keys = nz * 16

    def upper_part(h, j):
        request = (z * nx + j) * CORES + c
        mid = leaf_mid[request]
        root = mid_root[mid]
        query = qx[j, :, h * HEAD_DIM : (h + 1) * HEAD_DIM]
        root_scores = dot_nt(query, kv[h][0, :, root].reshape(keys, HEAD_DIM))
        mid_scores = dot_nt(query, kv[h][0, :, roots + mid].reshape(keys, HEAD_DIM))
        key = lax.broadcasted_iota(jnp.int32, mid_scores.shape, 1)
        key_pos = (key >> 4) * (nx * 16) + (key & 15) + x * 16
        root_scores = jnp.where(key_pos < upper_len[root], root_scores, NEG_FILL)
        mid_scores = jnp.where(key_pos < upper_len[roots + mid], mid_scores, NEG_FILL)
        o, lse = softmax_part(
            [
                (root_scores, kv[h][1, :, root].reshape(keys, HEAD_DIM)),
                (mid_scores, kv[h][1, :, roots + mid].reshape(keys, HEAD_DIM)),
            ]
        )
        row = col_to_row(lse)
        return o.astype(jnp.bfloat16), jnp.broadcast_to(row, (8, row.shape[1]))

    def upper_head(h):
        wait_bytes(kv[h].at[1 - c], sib_recv.at[h])

        @pl.loop(1, nx)
        def _(k):
            j = lax.rem(x + k, nx)
            o, lse = upper_part(h, j)
            o_send[h, j] = o
            s_send[h, j] = lse
            to = dev(z, j, c, y)
            send(s_send.at[h, j], s_recv.at[h, x], s_sem_s.at[h], s_sem_r.at[h], to)
            send(o_send.at[h, j], o_recv.at[h, x], o_sem_s.at[h], o_sem_r.at[h], to)

        o, lse = upper_part(h, x)
        o_recv[h, x] = o
        s_recv[h, x] = lse

    def merge_head(h):
        wait_bytes(s_recv.at[h, pl.ds(0, nx - 1)], s_sem_r.at[h])
        wait_bytes(o_recv.at[h, pl.ds(0, nx - 1)], o_sem_r.at[h])
        sums = [row_to_col(s_recv[h, i, 0:1, :], rows) for i in range(nx)]
        sums.append(leaf_lse[h][:, 0:1])
        top = functools.reduce(jnp.maximum, sums)
        total, weighted = 0.0, 0.0
        for i in range(nx + 1):
            weight = jnp.exp2(sums[i] - top)
            part = o_recv[h, i].astype(jnp.float32) if i < nx else leaf_o[h]
            total = total + weight
            weighted = weighted + weight * part
        attended = jnp.where(position < req_len[me], weighted / total, 0.0)
        at[h, y] = attended.astype(jnp.bfloat16)
        for k in range(1, ny):
            view = at.at[h, y]
            send(view, view, y_sem_s.at[h], y_sem_r.at[h], dev(z, x, c, y_mate(k)))

    def project_head(h):
        if h == 0:
            loads[8].wait()
            wait_bytes(w.at[pl.ds(0, ny - 1), pl.ds(0, half_rows)], wf_sem.at[1])
        wait_bytes(at.at[h, pl.ds(0, ny - 1)], y_sem_r.at[h])
        total = res[...].astype(jnp.float32) if h == 0 else acc[...]
        for i in range(ny):
            total = total + jnp.dot(
                at[h, i],
                w[i, h * HEAD_DIM : (h + 1) * HEAD_DIM, :],
                preferred_element_type=jnp.float32,
            )
        if h < heads - 1:
            acc[...] = total
        else:
            out[...] = total.astype(out.dtype)

    loads[7].wait()
    for i in range(heads + 2):
        if i < heads:
            upper_head(i)
        if 1 <= i <= heads:
            merge_head(i - 1)
        if i >= 2:
            project_head(i - 2)

    wait_bytes(up_other, pre_sem.at[0])
    wait_bytes(qx.at[pl.ds(0, nx - 1)], q_sem.at[0])
    wait_bytes(w.at[pl.ds(0, ny - 1), pl.ds(0, half_rows)], w_sem.at[0])
    wait_bytes(w.at[pl.ds(0, ny - 1), pl.ds(0, half_rows)], wf_sem.at[0])
    for h in range(heads):
        wait_bytes(kv[h].at[0, pl.ds(0, nz - 1)], ring_send.at[h])
        wait_bytes(kv[h].at[0], sib_send.at[h])
        wait_bytes(s_recv.at[h, pl.ds(0, nx - 1)], s_sem_s.at[h])
        wait_bytes(o_recv.at[h, pl.ds(0, nx - 1)], o_sem_s.at[h])
        wait_bytes(at.at[h, pl.ds(0, ny - 1)], y_sem_s.at[h])


def shards(
    nx,
    queries,
    new_keys,
    new_values,
    residual,
    w_out,
    leaf_keys,
    leaf_values,
    upper_keys,
    upper_values,
    req_len,
    leaf_mid,
    mid_root,
    upper_len,
    leaf_len,
):
    ny = lax.axis_size("grp")
    nz = lax.axis_size("tok") // (nx * CORES)
    rows, width = queries.shape
    heads = width // HEAD_DIM
    nodes, depth, _ = upper_keys.shape
    leaf_pos = leaf_keys.shape[1]
    roots = nodes - mid_root.shape[0]
    stat_width = -(-rows // 128) * 128
    bf16, f32 = jnp.bfloat16, jnp.float32
    dma = pltpu.SemaphoreType.DMA
    scratch = [pltpu.VMEM((2, nz, nodes, 16, HEAD_DIM), bf16) for _ in range(heads)]
    scratch += [
        pltpu.VMEM((2, nodes * depth, width), bf16),
        pltpu.VMEM((nodes * depth, width), bf16),
        pltpu.VMEM((nx, rows, width), bf16),
        pltpu.VMEM((leaf_pos, width), bf16),
        pltpu.VMEM((leaf_pos, width), bf16),
        pltpu.VMEM((rows, width), bf16),
        pltpu.VMEM((rows, width), bf16),
        pltpu.VMEM((rows, width), bf16),
        pltpu.VMEM((ny, width, width), bf16),
        pltpu.VMEM((heads, rows, HEAD_DIM), f32),
        pltpu.VMEM((heads, rows, HEAD_DIM), f32),
        pltpu.VMEM((heads, nx, rows, HEAD_DIM), bf16),
        pltpu.VMEM((heads, nx, rows, HEAD_DIM), bf16),
        pltpu.VMEM((heads, nx, 8, stat_width), f32),
        pltpu.VMEM((heads, nx, 8, stat_width), f32),
        pltpu.VMEM((heads, ny, rows, HEAD_DIM), bf16),
        pltpu.VMEM((rows, width), f32),
        dma((9,)),
        dma((2,)),
        dma((heads,)),
        dma((heads, 2, nz // 2)),
        dma((heads,)),
        dma((heads,)),
        dma((2,)),
        dma((2,)),
        dma((2,)),
        dma((heads,)),
        dma((heads,)),
        dma((heads,)),
        dma((heads,)),
        dma((heads,)),
        dma((heads,)),
    ]
    smem = pl.BlockSpec(memory_space=pltpu.SMEM)
    anyspace = pl.BlockSpec(memory_space=pl.ANY)
    return pl.pallas_call(
        functools.partial(kernel, nx, nz, ny, heads, roots),
        out_shape=jax.ShapeDtypeStruct((rows, width), bf16),
        in_specs=[smem] * 5 + [anyspace] * 9,
        out_specs=pl.BlockSpec(memory_space=pltpu.VMEM),
        scratch_shapes=scratch,
        compiler_params=pltpu.CompilerParams(
            collective_id=0, has_side_effects=True, vmem_limit_bytes=40 * 1024 * 1024
        ),
    )(
        req_len,
        leaf_mid,
        mid_root,
        upper_len,
        leaf_len,
        upper_keys.reshape(nodes * depth, width),
        upper_values.reshape(nodes * depth, width),
        queries,
        new_keys,
        new_values,
        residual,
        w_out,
        leaf_keys.reshape(leaf_pos, width),
        leaf_values.reshape(leaf_pos, width),
    )


def solution(mesh, nx=CHIPS_X):
    in_specs = (
        P("tok", "grp"),
        P("tok", "grp"),
        P("tok", "grp"),
        P("tok", "grp"),
        P("grp", None),
        P("tok", None, "grp"),
        P("tok", None, "grp"),
        P(None, "tok", "grp"),
        P(None, "tok", "grp"),
        P(),
        P(),
        P(),
        P(),
        P(),
    )
    return jax.shard_map(
        functools.partial(shards, nx),
        mesh=mesh,
        in_specs=in_specs,
        out_specs=P("tok", "grp"),
        check_vma=False,
    )
```

```python
import functools

import jax
import jax.numpy as jnp
from jax import lax
from jax.experimental import pallas as pl
from jax.experimental.pallas import tpu as pltpu
from jax.sharding import PartitionSpec as P

HEAD_DIM = 128
NEG_FILL = -1e30
LOG2E = 1.4426950408889634
CHIPS_X = 4
CORES = 2
SKEW = 0.5
MESH = pl.DeviceIdType.MESH


def dot_nt(a, b):
    return lax.dot_general(a, b, (((1,), (1,)), ((), ())), preferred_element_type=jnp.float32)


def wait_bytes(view, sem):
    pltpu.make_async_copy(view, view, sem).wait()


def col_to_row(col):
    pieces = []
    for start in range(0, col.shape[0], 128):
        piece = col[start : start + 128]
        n = piece.shape[0]
        diag = lax.broadcasted_iota(jnp.int32, (n, 128), 0) == lax.broadcasted_iota(
            jnp.int32, (n, 128), 1
        )
        spread = jnp.broadcast_to(piece, (n, 128))
        pieces.append(jnp.sum(jnp.where(diag, spread, 0.0), axis=0, keepdims=True))
    return jnp.concatenate(pieces, axis=1)


def row_to_col(row, n_rows):
    pieces = []
    for start in range(0, n_rows, 128):
        n = min(128, n_rows - start)
        diag = lax.broadcasted_iota(jnp.int32, (n, 128), 0) == lax.broadcasted_iota(
            jnp.int32, (n, 128), 1
        )
        spread = jnp.broadcast_to(row[:, start : start + 128], (n, 128))
        pieces.append(jnp.sum(jnp.where(diag, spread, 0.0), axis=1, keepdims=True))
    return jnp.concatenate(pieces, axis=0)


def softmax_part(parts):
    scale = HEAD_DIM ** (-0.5) * LOG2E
    top = functools.reduce(
        jnp.maximum, [jnp.max(s, axis=1, keepdims=True) for s, _ in parts]
    )
    total, weighted = 0.0, 0.0
    for s, v in parts:
        exps = jnp.exp2((s - top) * scale)
        total = total + jnp.sum(exps, axis=1, keepdims=True)
        weighted = weighted + jnp.dot(
            exps.astype(jnp.bfloat16), v, preferred_element_type=jnp.float32
        )
    return weighted / total, top * scale + jnp.log(total) * LOG2E


def kernel(
    nx,
    nz,
    ny,
    heads,
    roots,
    req_len_hbm,
    leaf_mid_hbm,
    mid_root_hbm,
    upper_len_hbm,
    leaf_len_hbm,
    uk,
    uv,
    q_hbm,
    nk_hbm,
    nv_hbm,
    res_hbm,
    w_hbm,
    lk_hbm,
    lv_hbm,
    out,
    *scratch,
):
    kv = scratch[:heads]
    (
        req_len,
        leaf_mid,
        mid_root,
        upper_len,
        leaf_len,
        up,
        up_other,
        qx,
        lk,
        lv,
        nk,
        nv,
        res,
        w,
        leaf_o,
        leaf_lse,
        o_send,
        o_recv,
        s_send,
        s_recv,
        at,
        acc,
        in_sem,
        pre_sem,
        ring_send,
        ring_recv,
        sib_send,
        sib_recv,
        q_sem,
        w_sem,
        wf_sem,
        o_sem_s,
        o_sem_r,
        s_sem_s,
        s_sem_r,
        y_sem_s,
        y_sem_r,
    ) = scratch[heads:]
    nodes = kv[0].shape[2]
    rows = qx.shape[1]
    width = heads * HEAD_DIM
    half_rows = width // CORES
    tok, y = lax.axis_index("tok"), lax.axis_index("grp")
    c = lax.rem(tok, CORES)
    x = lax.rem(lax.div(tok, CORES), nx)
    z = lax.div(tok, CORES * nx)

    def dev(z_, x_, c_, y_):
        return ((z_ * nx + x_) * CORES + c_, y_)

    sibling = dev(z, x, 1 - c, y)

    def z_mate(hops):
        return dev(lax.rem(z + nz + hops, nz), x, c, y)

    def x_mate(k):
        return lax.rem(x + k, nx)

    def y_mate(k):
        return lax.rem(y + k, ny)

    loads = [
        (uk, up.at[0]),
        (uv, up.at[1]),
        (q_hbm, qx.at[x]),
        (lk_hbm, lk),
        (lv_hbm, lv),
        (nk_hbm, nk),
        (nv_hbm, nv),
        (res_hbm, res),
        (w_hbm.at[:, pl.ds(pl.multiple_of(y * width, width), width)], w.at[y]),
        (req_len_hbm, req_len),
        (leaf_mid_hbm, leaf_mid),
        (mid_root_hbm, mid_root),
        (upper_len_hbm, upper_len),
        (leaf_len_hbm, leaf_len),
    ]
    loads = [pltpu.make_async_copy(a, b, in_sem.at[i]) for i, (a, b) in enumerate(loads)]
    for load in loads:
        load.start()

    partners = [sibling] + [z_mate(hops) for hops in (1, -1, 2, -2)]
    partners += [dev(z, x_mate(k), c, y) for k in range(1, nx)]
    partners += [dev(z, x, c, y_mate(k)) for k in range(1, ny)]
    barrier = pltpu.get_barrier_semaphore()
    for partner in partners:
        pl.semaphore_signal(barrier, inc=1, device_id=partner, device_id_type=MESH)
    pl.semaphore_wait(barrier, len(partners))

    def send(src, dst, send_sem, recv_sem, device):
        pltpu.make_async_remote_copy(
            src_ref=src,
            dst_ref=dst,
            send_sem=send_sem,
            recv_sem=recv_sem,
            device_id=device,
            device_id_type=MESH,
        ).start()

    loads[0].wait()
    loads[1].wait()
    send(up.at[1 - c], up_other, pre_sem.at[0], pre_sem.at[1], sibling)
    for k in range(1, nx):
        send(q_hbm, qx.at[x], q_sem.at[0], q_sem.at[1], dev(z, x_mate(k), c, y))
    my_half = pl.ds(pl.multiple_of(c * half_rows, half_rows), half_rows)
    for k in range(1, ny):
        to = y_mate(k)
        send(
            w_hbm.at[my_half, pl.ds(pl.multiple_of(to * width, width), width)],
            w.at[y, my_half],
            w_sem.at[0],
            w_sem.at[1],
            dev(z, x, c, to),
        )
    wait_bytes(up_other, pre_sem.at[1])
    mine = up[c].astype(jnp.float32).reshape(nodes, 8, width)
    other = up_other[...].astype(jnp.float32).reshape(nodes, 8, width)
    first = jnp.where(c == 0, mine, other)
    second = jnp.where(c == 0, other, mine)
    block = jnp.concatenate([first, second], axis=1).astype(jnp.bfloat16)
    for h in range(heads):
        kv[h][c, z] = block[:, :, h * HEAD_DIM : (h + 1) * HEAD_DIM]

    far = nz // 2
    stages = -(-far // 2)
    cut = nodes // 2

    def z_view(h, direction, distance):
        return kv[h].at[c, lax.rem(z + (nz - distance if direction == 0 else distance), nz)]

    def z_part(h, direction, held, distance):
        view = z_view(h, direction, held)
        if distance == far:
            view = view.at[pl.ds(0, cut)] if direction == 0 else view.at[pl.ds(cut, nodes - cut)]
        return view

    def z_start(h, stage):
        for hops in (2, 1):
            for direction in range(2):
                distance = 2 * stage + hops
                if distance <= far:
                    view = z_part(h, direction, 2 * stage, distance)
                    send(
                        view,
                        view,
                        ring_send.at[h],
                        ring_recv.at[h, direction, distance - 1],
                        z_mate(hops if direction == 0 else -hops),
                    )

    def z_wait(h, direction, distance):
        wait_bytes(
            z_part(h, direction, distance, distance), ring_recv.at[h, direction, distance - 1]
        )

    def share(h, view):
        send(view, view, sib_send.at[h], sib_recv.at[h], sibling)

    def z_stage(h, stage):
        if stage == 0:
            z_start(h, 0)
            share(h, kv[h].at[c, z])
            return
        for direction in range(2):
            z_wait(h, direction, 2 * stage)
        z_start(h, stage)
        for direction in range(2):
            share(h, z_view(h, direction, 2 * stage))
        for direction in range(2):
            z_wait(h, direction, 2 * stage - 1)
            share(h, z_view(h, direction, 2 * stage - 1))

    def z_finish(h):
        for distance in range(2 * stages - 1, far + 1):
            for direction in range(2):
                z_wait(h, direction, distance)
                if distance < far:
                    share(h, z_view(h, direction, distance))
        share(h, z_view(h, 0, far))

    me = tok
    position = lax.broadcasted_iota(jnp.int32, (rows, 1), 0)

    def leaf_part(h):
        cols = slice(h * HEAD_DIM, (h + 1) * HEAD_DIM)
        query = qx[x, :, cols]
        leaf_scores = dot_nt(query, lk[:, cols])
        at_pos = lax.broadcasted_iota(jnp.int32, leaf_scores.shape, 1)
        leaf_scores = jnp.where(at_pos < leaf_len[me], leaf_scores, NEG_FILL)
        new_scores = dot_nt(query, nk[:, cols])
        key_pos = lax.broadcasted_iota(jnp.int32, new_scores.shape, 1)
        query_pos = lax.broadcasted_iota(jnp.int32, new_scores.shape, 0)
        allowed = (key_pos <= query_pos) & (key_pos < req_len[me])
        new_scores = jnp.where(allowed, new_scores, NEG_FILL)
        o, lse = softmax_part([(leaf_scores, lv[:, cols]), (new_scores, nv[:, cols])])
        leaf_o[h] = o
        leaf_lse[h] = jnp.broadcast_to(lse, (rows, HEAD_DIM))

    def leaf_head(h):
        if h == 0:
            for load in loads[2:7] + loads[9:]:
                load.wait()
        leaf_part(h)

    def share_w():
        wait_bytes(w.at[pl.ds(0, ny - 1), pl.ds(0, half_rows)], w_sem.at[1])
        for k in range(1, ny):
            view = w.at[y_mate(k), my_half]
            send(view, view, wf_sem.at[0], wf_sem.at[1], sibling)

    keys = nz * 16

    def upper_part(h, j):
        request = (z * nx + j) * CORES + c
        mid = leaf_mid[request]
        root = mid_root[mid]
        query = qx[j, :, h * HEAD_DIM : (h + 1) * HEAD_DIM]
        root_scores = dot_nt(query, kv[h][0, :, root].reshape(keys, HEAD_DIM))
        mid_scores = dot_nt(query, kv[h][0, :, roots + mid].reshape(keys, HEAD_DIM))
        key = lax.broadcasted_iota(jnp.int32, mid_scores.shape, 1)
        key_pos = (key >> 4) * (nx * 16) + (key & 15) + x * 16
        root_scores = jnp.where(key_pos < upper_len[root], root_scores, NEG_FILL)
        mid_scores = jnp.where(key_pos < upper_len[roots + mid], mid_scores, NEG_FILL)
        o, lse = softmax_part(
            [
                (root_scores, kv[h][1, :, root].reshape(keys, HEAD_DIM)),
                (mid_scores, kv[h][1, :, roots + mid].reshape(keys, HEAD_DIM)),
            ]
        )
        row = col_to_row(lse)
        return o.astype(jnp.bfloat16), jnp.broadcast_to(row, (8, row.shape[1]))

    def upper_head(h):
        if h == 0:
            wait_bytes(qx.at[pl.ds(0, nx - 1)], q_sem.at[1])
        wait_bytes(kv[h].at[1 - c], sib_recv.at[h])

        @pl.loop(1, nx)
        def _(k):
            j = lax.rem(x + k, nx)
            o, lse = upper_part(h, j)
            o_send[h, j] = o
            s_send[h, j] = lse
            to = dev(z, j, c, y)
            send(s_send.at[h, j], s_recv.at[h, x], s_sem_s.at[h], s_sem_r.at[h], to)
            send(o_send.at[h, j], o_recv.at[h, x], o_sem_s.at[h], o_sem_r.at[h], to)

        o, lse = upper_part(h, x)
        o_recv[h, x] = o
        s_recv[h, x] = lse

    def merge_head(h):
        wait_bytes(s_recv.at[h, pl.ds(0, nx - 1)], s_sem_r.at[h])
        wait_bytes(o_recv.at[h, pl.ds(0, nx - 1)], o_sem_r.at[h])
        sums = [row_to_col(s_recv[h, i, 0:1, :], rows) for i in range(nx)]
        sums.append(leaf_lse[h][:, 0:1])
        top = functools.reduce(jnp.maximum, sums)
        total, weighted = 0.0, 0.0
        for i in range(nx + 1):
            weight = jnp.exp2(sums[i] - top)
            part = o_recv[h, i].astype(jnp.float32) if i < nx else leaf_o[h]
            total = total + weight
            weighted = weighted + weight * part
        attended = jnp.where(position < req_len[me], weighted / total, 0.0)
        at[h, y] = attended.astype(jnp.bfloat16)
        for k in range(1, ny):
            view = at.at[h, y]
            send(view, view, y_sem_s.at[h], y_sem_r.at[h], dev(z, x, c, y_mate(k)))

    def project_head(h):
        if h == 0:
            loads[8].wait()
            wait_bytes(w.at[pl.ds(0, ny - 1), pl.ds(0, half_rows)], wf_sem.at[1])
        wait_bytes(at.at[h, pl.ds(0, ny - 1)], y_sem_r.at[h])
        total = res[...].astype(jnp.float32) if h == 0 else acc[...]
        for i in range(ny):
            total = total + jnp.dot(
                at[h, i],
                w[i, h * HEAD_DIM : (h + 1) * HEAD_DIM, :],
                preferred_element_type=jnp.float32,
            )
        if h < heads - 1:
            acc[...] = total
        else:
            out[...] = total.astype(out.dtype)

    events = [(stages - 0.6, share_w)]
    for h in range(heads):
        for stage in range(stages):
            events.append((stage + SKEW * h, functools.partial(z_stage, h, stage)))
        end = stages + SKEW * h
        events.append((0.6 + 0.5 * h, functools.partial(leaf_head, h)))
        events.append((end, functools.partial(z_finish, h)))
        events.append((end + 0.4, functools.partial(upper_head, h)))
        events.append((end + 1.6, functools.partial(merge_head, h)))
        events.append((end + 2.8, functools.partial(project_head, h)))
    loads[7].wait()
    for _, event in sorted(events, key=lambda item: item[0]):
        event()

    wait_bytes(up_other, pre_sem.at[0])
    wait_bytes(qx.at[pl.ds(0, nx - 1)], q_sem.at[0])
    wait_bytes(w.at[pl.ds(0, ny - 1), pl.ds(0, half_rows)], w_sem.at[0])
    wait_bytes(w.at[pl.ds(0, ny - 1), pl.ds(0, half_rows)], wf_sem.at[0])
    for h in range(heads):
        wait_bytes(kv[h].at[0, pl.ds(0, nz - 1)], ring_send.at[h])
        wait_bytes(kv[h].at[0], sib_send.at[h])
        wait_bytes(s_recv.at[h, pl.ds(0, nx - 1)], s_sem_s.at[h])
        wait_bytes(o_recv.at[h, pl.ds(0, nx - 1)], o_sem_s.at[h])
        wait_bytes(at.at[h, pl.ds(0, ny - 1)], y_sem_s.at[h])


def shards(
    nx,
    queries,
    new_keys,
    new_values,
    residual,
    w_out,
    leaf_keys,
    leaf_values,
    upper_keys,
    upper_values,
    req_len,
    leaf_mid,
    mid_root,
    upper_len,
    leaf_len,
):
    ny = lax.axis_size("grp")
    nz = lax.axis_size("tok") // (nx * CORES)
    rows, width = queries.shape
    heads = width // HEAD_DIM
    nodes, depth, _ = upper_keys.shape
    leaf_pos = leaf_keys.shape[1]
    roots = nodes - mid_root.shape[0]
    stat_width = -(-rows // 128) * 128
    bf16, f32 = jnp.bfloat16, jnp.float32
    dma = pltpu.SemaphoreType.DMA
    scratch = [pltpu.VMEM((2, nz, nodes, 16, HEAD_DIM), bf16) for _ in range(heads)]
    scratch += [pltpu.SMEM(a.shape, a.dtype) for a in (req_len, leaf_mid, mid_root, upper_len, leaf_len)]
    scratch += [
        pltpu.VMEM((2, nodes * depth, width), bf16),
        pltpu.VMEM((nodes * depth, width), bf16),
        pltpu.VMEM((nx, rows, width), bf16),
        pltpu.VMEM((leaf_pos, width), bf16),
        pltpu.VMEM((leaf_pos, width), bf16),
        pltpu.VMEM((rows, width), bf16),
        pltpu.VMEM((rows, width), bf16),
        pltpu.VMEM((rows, width), bf16),
        pltpu.VMEM((ny, width, width), bf16),
        pltpu.VMEM((heads, rows, HEAD_DIM), f32),
        pltpu.VMEM((heads, rows, HEAD_DIM), f32),
        pltpu.VMEM((heads, nx, rows, HEAD_DIM), bf16),
        pltpu.VMEM((heads, nx, rows, HEAD_DIM), bf16),
        pltpu.VMEM((heads, nx, 8, stat_width), f32),
        pltpu.VMEM((heads, nx, 8, stat_width), f32),
        pltpu.VMEM((heads, ny, rows, HEAD_DIM), bf16),
        pltpu.VMEM((rows, width), f32),
        dma((14,)),
        dma((2,)),
        dma((heads,)),
        dma((heads, 2, nz // 2)),
        dma((heads,)),
        dma((heads,)),
        dma((2,)),
        dma((2,)),
        dma((2,)),
        dma((heads,)),
        dma((heads,)),
        dma((heads,)),
        dma((heads,)),
        dma((heads,)),
        dma((heads,)),
    ]
    hbm = pl.BlockSpec(memory_space=pltpu.HBM)
    return pl.pallas_call(
        functools.partial(kernel, nx, nz, ny, heads, roots),
        out_shape=jax.ShapeDtypeStruct((rows, width), bf16),
        in_specs=[hbm] * 14,
        out_specs=pl.BlockSpec(memory_space=pltpu.VMEM),
        scratch_shapes=scratch,
        compiler_params=pltpu.CompilerParams(
            collective_id=0, has_side_effects=True, vmem_limit_bytes=63 * 1024 * 1024
        ),
    )(
        req_len,
        leaf_mid,
        mid_root,
        upper_len,
        leaf_len,
        upper_keys.reshape(nodes * depth, width),
        upper_values.reshape(nodes * depth, width),
        queries,
        new_keys,
        new_values,
        residual,
        w_out,
        leaf_keys.reshape(leaf_pos, width),
        leaf_values.reshape(leaf_pos, width),
    )


def solution(mesh, nx=CHIPS_X):
    in_specs = (
        P("tok", "grp"),
        P("tok", "grp"),
        P("tok", "grp"),
        P("tok", "grp"),
        P("grp", None),
        P("tok", None, "grp"),
        P("tok", None, "grp"),
        P(None, "tok", "grp"),
        P(None, "tok", "grp"),
        P(),
        P(),
        P(),
        P(),
        P(),
    )
    return jax.shard_map(
        functools.partial(shards, nx),
        mesh=mesh,
        in_specs=in_specs,
        out_specs=P("tok", "grp"),
        check_vma=False,
    )
```

```python
import functools

import jax
import jax.numpy as jnp
from jax import lax
from jax.experimental import pallas as pl
from jax.experimental.pallas import tpu as pltpu
from jax.sharding import PartitionSpec as P

HEAD_DIM = 128
NEG_FILL = -1e30
LOG2E = 1.4426950408889634
CHIPS_X = 4
CORES = 2
OFFSETS = (0, 0.7, 1.4, 2.1)
Q_AT, W_FROM = 0.02, 1.6
Z_SKIPS = (4, 4, 4, 4)
W_AT, UPPER_AT, MERGE_AT, PROJECT_AT = 3.4, 0.4, 1.6, 2.8
MESH = pl.DeviceIdType.MESH


def dot_nt(a, b):
    return lax.dot_general(a, b, (((1,), (1,)), ((), ())), preferred_element_type=jnp.float32)


def wait_bytes(view, sem):
    pltpu.make_async_copy(view, view, sem).wait()


def col_to_row(col):
    pieces = []
    for start in range(0, col.shape[0], 128):
        piece = col[start : start + 128]
        n = piece.shape[0]
        diag = lax.broadcasted_iota(jnp.int32, (n, 128), 0) == lax.broadcasted_iota(
            jnp.int32, (n, 128), 1
        )
        spread = jnp.broadcast_to(piece, (n, 128))
        pieces.append(jnp.sum(jnp.where(diag, spread, 0.0), axis=0, keepdims=True))
    return jnp.concatenate(pieces, axis=1)


def row_to_col(row, n_rows):
    pieces = []
    for start in range(0, n_rows, 128):
        n = min(128, n_rows - start)
        diag = lax.broadcasted_iota(jnp.int32, (n, 128), 0) == lax.broadcasted_iota(
            jnp.int32, (n, 128), 1
        )
        spread = jnp.broadcast_to(row[:, start : start + 128], (n, 128))
        pieces.append(jnp.sum(jnp.where(diag, spread, 0.0), axis=1, keepdims=True))
    return jnp.concatenate(pieces, axis=0)


def z_plan(far, skips):
    plan, held = [], 0
    while held < far:
        hops = 2 if len(plan) < skips and held + 2 <= far else 1
        plan.append([(held, n) for n in range(hops, 0, -1)])
        held += hops
    return plan


def softmax_part(parts):
    scale = HEAD_DIM ** (-0.5) * LOG2E
    top = functools.reduce(
        jnp.maximum, [jnp.max(s, axis=1, keepdims=True) for s, _ in parts]
    )
    total, weighted = 0.0, 0.0
    for s, v in parts:
        exps = jnp.exp2((s - top) * scale)
        total = total + jnp.sum(exps, axis=1, keepdims=True)
        weighted = weighted + jnp.dot(
            exps.astype(jnp.bfloat16), v, preferred_element_type=jnp.float32
        )
    return weighted / total, top * scale + jnp.log(total) * LOG2E


def kernel(
    nx,
    nz,
    ny,
    heads,
    roots,
    z_skips,
    req_len_hbm,
    leaf_mid_hbm,
    mid_root_hbm,
    upper_len_hbm,
    leaf_len_hbm,
    uk,
    uv,
    q_hbm,
    nk_hbm,
    nv_hbm,
    res_hbm,
    w_hbm,
    lk_hbm,
    lv_hbm,
    out,
    *scratch,
):
    kv = scratch[:heads]
    (
        req_len,
        leaf_mid,
        mid_root,
        upper_len,
        leaf_len,
        up,
        qx,
        lk,
        lv,
        nk,
        nv,
        res,
        w,
        leaf_o,
        leaf_lse,
        o_send,
        o_recv,
        s_send,
        s_recv,
        at,
        acc,
        in_sem,
        ring_send,
        ring_recv,
        sib_send,
        sib_recv,
        q_sem,
        w_sem,
        wf_sem,
        o_sem_s,
        o_sem_r,
        s_sem_s,
        s_sem_r,
        y_sem_s,
        y_sem_r,
    ) = scratch[heads:]
    nodes = kv[0].shape[2]
    rows = qx.shape[1]
    width = heads * HEAD_DIM
    half_rows = width // CORES
    tok, y = lax.axis_index("tok"), lax.axis_index("grp")
    c = lax.rem(tok, CORES)
    x = lax.rem(lax.div(tok, CORES), nx)
    z = lax.div(tok, CORES * nx)

    def dev(z_, x_, c_, y_):
        return ((z_ * nx + x_) * CORES + c_, y_)

    sibling = dev(z, x, 1 - c, y)

    def z_mate(hops):
        return dev(lax.rem(z + nz + hops, nz), x, c, y)

    def x_mate(k):
        return lax.rem(x + k, nx)

    def y_mate(k):
        return lax.rem(y + k, ny)

    loads = [
        (uk, up.at[0]),
        (uv, up.at[1]),
        (q_hbm, qx.at[x]),
        (lk_hbm, lk),
        (lv_hbm, lv),
        (nk_hbm, nk),
        (nv_hbm, nv),
        (res_hbm, res),
        (w_hbm.at[:, pl.ds(pl.multiple_of(y * width, width), width)], w.at[y]),
        (req_len_hbm, req_len),
        (leaf_mid_hbm, leaf_mid),
        (mid_root_hbm, mid_root),
        (upper_len_hbm, upper_len),
        (leaf_len_hbm, leaf_len),
    ]
    loads = [pltpu.make_async_copy(a, b, in_sem.at[i]) for i, (a, b) in enumerate(loads)]
    for load in loads:
        load.start()

    partners = [sibling] + [z_mate(hops) for hops in (1, -1, 2, -2)]
    partners += [dev(z, x_mate(k), c, y) for k in range(1, nx)]
    partners += [dev(z, x, c, y_mate(k)) for k in range(1, ny)]
    barrier = pltpu.get_barrier_semaphore()
    for partner in partners:
        pl.semaphore_signal(barrier, inc=1, device_id=partner, device_id_type=MESH)
    loads[0].wait()
    loads[1].wait()
    block = jnp.concatenate(
        [up[i].astype(jnp.float32).reshape(nodes, 8, width) for i in range(2)], axis=1
    ).astype(jnp.bfloat16)
    for h in range(heads):
        kv[h][c, z] = block[:, :, h * HEAD_DIM : (h + 1) * HEAD_DIM]
    pl.semaphore_wait(barrier, len(partners))

    def send(src, dst, send_sem, recv_sem, device):
        pltpu.make_async_remote_copy(
            src_ref=src,
            dst_ref=dst,
            send_sem=send_sem,
            recv_sem=recv_sem,
            device_id=device,
            device_id_type=MESH,
        ).start()

    my_half = pl.ds(pl.multiple_of(c * half_rows, half_rows), half_rows)

    def send_queries():
        for k in sorted(range(1, nx), key=lambda k: -min(k, nx - k)):
            send(q_hbm, qx.at[x], q_sem.at[0], q_sem.at[1], dev(z, x_mate(k), c, y))

    def send_w():
        for k in range(1, ny):
            to = y_mate(k)
            send(
                w_hbm.at[my_half, pl.ds(pl.multiple_of(to * width, width), width)],
                w.at[y, my_half],
                w_sem.at[0],
                w_sem.at[1],
                dev(z, x, c, to),
            )

    far = nz // 2
    cut = nodes // 2

    def z_view(h, direction, distance):
        return kv[h].at[c, lax.rem(z + (nz - distance if direction == 0 else distance), nz)]

    def z_part(h, direction, held, distance):
        view = z_view(h, direction, held)
        if distance == far:
            view = view.at[pl.ds(0, cut)] if direction == 0 else view.at[pl.ds(cut, nodes - cut)]
        return view

    def z_wait(h, direction, distance):
        wait_bytes(
            z_part(h, direction, distance, distance), ring_recv.at[h, direction, distance - 1]
        )

    def share(h, view):
        send(view, view, sib_send.at[h], sib_recv.at[h], sibling)

    plans = [z_plan(far, z_skips[min(h, len(z_skips) - 1)]) for h in range(heads)]

    def z_stage(h, stage):
        came = [0] if stage == 0 else [held + hops for held, hops in plans[h][stage - 1]]
        go_on = sorted({held for held, _ in plans[h][stage]}) if stage < len(plans[h]) else []
        for held in go_on:
            if held:
                for direction in range(2):
                    z_wait(h, direction, held)
        for held, hops in plans[h][stage] if stage < len(plans[h]) else ():
            for direction in range(2):
                view = z_part(h, direction, held, held + hops)
                send(
                    view,
                    view,
                    ring_send.at[h],
                    ring_recv.at[h, direction, held + hops - 1],
                    z_mate(hops if direction == 0 else -hops),
                )
        for distance in sorted(came, key=lambda d: d not in go_on):
            if distance == 0:
                share(h, kv[h].at[c, z])
                continue
            for direction in range(2):
                if distance not in go_on:
                    z_wait(h, direction, distance)
                if distance < far:
                    share(h, z_view(h, direction, distance))
            if distance == far:
                share(h, z_view(h, 0, far))

    me = tok
    position = lax.broadcasted_iota(jnp.int32, (rows, 1), 0)

    def leaf_part(h):
        cols = slice(h * HEAD_DIM, (h + 1) * HEAD_DIM)
        query = qx[x, :, cols]
        leaf_scores = dot_nt(query, lk[:, cols])
        at_pos = lax.broadcasted_iota(jnp.int32, leaf_scores.shape, 1)
        leaf_scores = jnp.where(at_pos < leaf_len[me], leaf_scores, NEG_FILL)
        new_scores = dot_nt(query, nk[:, cols])
        key_pos = lax.broadcasted_iota(jnp.int32, new_scores.shape, 1)
        query_pos = lax.broadcasted_iota(jnp.int32, new_scores.shape, 0)
        allowed = (key_pos <= query_pos) & (key_pos < req_len[me])
        new_scores = jnp.where(allowed, new_scores, NEG_FILL)
        o, lse = softmax_part([(leaf_scores, lv[:, cols]), (new_scores, nv[:, cols])])
        leaf_o[h] = o
        leaf_lse[h] = jnp.broadcast_to(lse, (rows, HEAD_DIM))

    def leaf_head(h):
        if h == 0:
            for load in loads[2:7] + loads[9:]:
                load.wait()
        leaf_part(h)

    def share_w():
        wait_bytes(w.at[pl.ds(0, ny - 1), pl.ds(0, half_rows)], w_sem.at[1])
        for k in range(1, ny):
            view = w.at[y_mate(k), my_half]
            send(view, view, wf_sem.at[0], wf_sem.at[1], sibling)

    keys = nz * 16

    def upper_part(h, j):
        request = (z * nx + j) * CORES + c
        mid = leaf_mid[request]
        root = mid_root[mid]
        query = qx[j, :, h * HEAD_DIM : (h + 1) * HEAD_DIM]

        def rows_of(node):
            both = kv[h][:, :, node].astype(jnp.float32).reshape(keys // 8, 16, HEAD_DIM)
            return (
                both[:, :8].reshape(keys, HEAD_DIM).astype(jnp.bfloat16),
                both[:, 8:].reshape(keys, HEAD_DIM).astype(jnp.bfloat16),
            )

        root_keys, root_values = rows_of(root)
        mid_keys, mid_values = rows_of(roots + mid)
        root_scores = dot_nt(query, root_keys)
        mid_scores = dot_nt(query, mid_keys)
        key = lax.broadcasted_iota(jnp.int32, mid_scores.shape, 1)
        core = (key >= keys // 2).astype(jnp.int32)
        key = key - core * (keys // 2)
        key_pos = (key >> 3) * (nx * 16) + x * 16 + core * 8 + (key & 7)
        root_scores = jnp.where(key_pos < upper_len[root], root_scores, NEG_FILL)
        mid_scores = jnp.where(key_pos < upper_len[roots + mid], mid_scores, NEG_FILL)
        o, lse = softmax_part([(root_scores, root_values), (mid_scores, mid_values)])
        row = col_to_row(lse)
        return o.astype(jnp.bfloat16), jnp.broadcast_to(row, (8, row.shape[1]))

    def upper_head(h):
        if h == 0:
            wait_bytes(qx.at[pl.ds(0, nx - 1)], q_sem.at[1])
        wait_bytes(kv[h].at[1 - c], sib_recv.at[h])

        @pl.loop(0, nx - 1)
        def _(k):
            j = lax.rem(x + lax.rem(k + nx // 2 - 1, nx - 1) + 1, nx)
            o, lse = upper_part(h, j)
            o_send[h, j] = o
            s_send[h, j] = lse
            to = dev(z, j, c, y)
            send(s_send.at[h, j], s_recv.at[h, x], s_sem_s.at[h], s_sem_r.at[h], to)
            send(o_send.at[h, j], o_recv.at[h, x], o_sem_s.at[h], o_sem_r.at[h], to)

        o, lse = upper_part(h, x)
        o_recv[h, x] = o
        s_recv[h, x] = lse

    def merge_head(h):
        wait_bytes(s_recv.at[h, pl.ds(0, nx - 1)], s_sem_r.at[h])
        wait_bytes(o_recv.at[h, pl.ds(0, nx - 1)], o_sem_r.at[h])
        sums = [row_to_col(s_recv[h, i, 0:1, :], rows) for i in range(nx)]
        sums.append(leaf_lse[h][:, 0:1])
        top = functools.reduce(jnp.maximum, sums)
        total, weighted = 0.0, 0.0
        for i in range(nx + 1):
            weight = jnp.exp2(sums[i] - top)
            part = o_recv[h, i].astype(jnp.float32) if i < nx else leaf_o[h]
            total = total + weight
            weighted = weighted + weight * part
        attended = jnp.where(position < req_len[me], weighted / total, 0.0)
        at[h, y] = attended.astype(jnp.bfloat16)
        for k in sorted(range(1, ny), key=lambda k: -min(k, ny - k)):
            view = at.at[h, y]
            send(view, view, y_sem_s.at[h], y_sem_r.at[h], dev(z, x, c, y_mate(k)))

    def project_head(h):
        if h == 0:
            loads[8].wait()
            wait_bytes(w.at[pl.ds(0, ny - 1), pl.ds(0, half_rows)], wf_sem.at[1])
        wait_bytes(at.at[h, pl.ds(0, ny - 1)], y_sem_r.at[h])
        total = res[...].astype(jnp.float32) if h == 0 else acc[...]
        for i in range(ny):
            total = total + jnp.dot(
                at[h, i],
                w[i, h * HEAD_DIM : (h + 1) * HEAD_DIM, :],
                preferred_element_type=jnp.float32,
            )
        if h < heads - 1:
            acc[...] = total
        else:
            out[...] = total.astype(out.dtype)

    events = [(Q_AT, send_queries), (W_FROM, send_w), (W_AT, share_w)]
    for h in range(heads):
        for stage in range(len(plans[h]) + 1):
            events.append((stage + OFFSETS[h], functools.partial(z_stage, h, stage)))
        end = len(plans[h]) + OFFSETS[h]
        events.append((0.6 + 0.5 * h, functools.partial(leaf_head, h)))
        events.append((end + UPPER_AT, functools.partial(upper_head, h)))
        events.append((end + MERGE_AT, functools.partial(merge_head, h)))
        events.append((end + PROJECT_AT, functools.partial(project_head, h)))
    loads[7].wait()
    for _, event in sorted(events, key=lambda item: item[0]):
        event()

    wait_bytes(qx.at[pl.ds(0, nx - 1)], q_sem.at[0])
    wait_bytes(w.at[pl.ds(0, ny - 1), pl.ds(0, half_rows)], w_sem.at[0])
    wait_bytes(w.at[pl.ds(0, ny - 1), pl.ds(0, half_rows)], wf_sem.at[0])
    for h in range(heads):
        wait_bytes(kv[h].at[0, pl.ds(0, nz - 1)], ring_send.at[h])
        wait_bytes(kv[h].at[0], sib_send.at[h])
        wait_bytes(s_recv.at[h, pl.ds(0, nx - 1)], s_sem_s.at[h])
        wait_bytes(o_recv.at[h, pl.ds(0, nx - 1)], o_sem_s.at[h])
        wait_bytes(at.at[h, pl.ds(0, ny - 1)], y_sem_s.at[h])


def shards(
    nx,
    queries,
    new_keys,
    new_values,
    residual,
    w_out,
    leaf_keys,
    leaf_values,
    upper_keys,
    upper_values,
    req_len,
    leaf_mid,
    mid_root,
    upper_len,
    leaf_len,
):
    ny = lax.axis_size("grp")
    nz = lax.axis_size("tok") // (nx * CORES)
    rows, width = queries.shape
    heads = width // HEAD_DIM
    nodes, depth, _ = upper_keys.shape
    leaf_pos = leaf_keys.shape[1]
    roots = nodes - mid_root.shape[0]
    stat_width = -(-rows // 128) * 128
    bf16, f32 = jnp.bfloat16, jnp.float32
    dma = pltpu.SemaphoreType.DMA
    scratch = [pltpu.VMEM((2, nz, nodes, 16, HEAD_DIM), bf16) for _ in range(heads)]
    scratch += [pltpu.SMEM(a.shape, a.dtype) for a in (req_len, leaf_mid, mid_root, upper_len, leaf_len)]
    scratch += [
        pltpu.VMEM((2, nodes * depth, width), bf16),
        pltpu.VMEM((nx, rows, width), bf16),
        pltpu.VMEM((leaf_pos, width), bf16),
        pltpu.VMEM((leaf_pos, width), bf16),
        pltpu.VMEM((rows, width), bf16),
        pltpu.VMEM((rows, width), bf16),
        pltpu.VMEM((rows, width), bf16),
        pltpu.VMEM((ny, width, width), bf16),
        pltpu.VMEM((heads, rows, HEAD_DIM), f32),
        pltpu.VMEM((heads, rows, HEAD_DIM), f32),
        pltpu.VMEM((heads, nx, rows, HEAD_DIM), bf16),
        pltpu.VMEM((heads, nx, rows, HEAD_DIM), bf16),
        pltpu.VMEM((heads, nx, 8, stat_width), f32),
        pltpu.VMEM((heads, nx, 8, stat_width), f32),
        pltpu.VMEM((heads, ny, rows, HEAD_DIM), bf16),
        pltpu.VMEM((rows, width), f32),
        dma((14,)),
        dma((heads,)),
        dma((heads, 2, nz // 2)),
        dma((heads,)),
        dma((heads,)),
        dma((2,)),
        dma((2,)),
        dma((2,)),
        dma((heads,)),
        dma((heads,)),
        dma((heads,)),
        dma((heads,)),
        dma((heads,)),
        dma((heads,)),
    ]
    hbm = pl.BlockSpec(memory_space=pltpu.HBM)
    return pl.pallas_call(
        functools.partial(kernel, nx, nz, ny, heads, roots, Z_SKIPS),
        out_shape=jax.ShapeDtypeStruct((rows, width), bf16),
        in_specs=[hbm] * 14,
        out_specs=pl.BlockSpec(memory_space=pltpu.VMEM),
        scratch_shapes=scratch,
        compiler_params=pltpu.CompilerParams(
            collective_id=0, has_side_effects=True, vmem_limit_bytes=63 * 1024 * 1024
        ),
    )(
        req_len,
        leaf_mid,
        mid_root,
        upper_len,
        leaf_len,
        upper_keys.reshape(nodes * depth, width),
        upper_values.reshape(nodes * depth, width),
        queries,
        new_keys,
        new_values,
        residual,
        w_out,
        leaf_keys.reshape(leaf_pos, width),
        leaf_values.reshape(leaf_pos, width),
    )


def solution(mesh, nx=CHIPS_X):
    in_specs = (
        P("tok", "grp"),
        P("tok", "grp"),
        P("tok", "grp"),
        P("tok", "grp"),
        P("grp", None),
        P("tok", None, "grp"),
        P("tok", None, "grp"),
        P(None, "tok", "grp"),
        P(None, "tok", "grp"),
        P(),
        P(),
        P(),
        P(),
        P(),
    )
    return jax.shard_map(
        functools.partial(shards, nx),
        mesh=mesh,
        in_specs=in_specs,
        out_specs=P("tok", "grp"),
        check_vma=False,
    )
```

```python
import functools

import jax
import jax.numpy as jnp
from jax import lax
from jax.experimental import pallas as pl
from jax.experimental.pallas import tpu as pltpu
from jax.sharding import PartitionSpec as P

HEAD_DIM = 128
NEG_FILL = -1e30
LOG2E = 1.4426950408889634
CHIPS_X = 4
CORES = 2
OFFSETS = (0, 0.7, 1.4, 2.1)
LEAF_AT = (0.75, 0.8, 0.85, 0.9)
Q_AT, W_FROM = 0.02, 1.6
Z_SKIPS = (4, 4, 4, 4)
W_AT, UPPER_AT, MERGE_AT, PROJECT_AT = 3.4, 0.4, 1.6, 2.8
MESH = pl.DeviceIdType.MESH


def dot_nt(a, b):
    return lax.dot_general(a, b, (((1,), (1,)), ((), ())), preferred_element_type=jnp.float32)


def wait_bytes(view, sem):
    pltpu.make_async_copy(view, view, sem).wait()


def col_to_row(col):
    pieces = []
    for start in range(0, col.shape[0], 128):
        piece = col[start : start + 128]
        n = piece.shape[0]
        diag = lax.broadcasted_iota(jnp.int32, (n, 128), 0) == lax.broadcasted_iota(
            jnp.int32, (n, 128), 1
        )
        spread = jnp.broadcast_to(piece, (n, 128))
        pieces.append(jnp.sum(jnp.where(diag, spread, 0.0), axis=0, keepdims=True))
    return jnp.concatenate(pieces, axis=1)


def row_to_col(row, n_rows):
    pieces = []
    for start in range(0, n_rows, 128):
        n = min(128, n_rows - start)
        diag = lax.broadcasted_iota(jnp.int32, (n, 128), 0) == lax.broadcasted_iota(
            jnp.int32, (n, 128), 1
        )
        spread = jnp.broadcast_to(row[:, start : start + 128], (n, 128))
        pieces.append(jnp.sum(jnp.where(diag, spread, 0.0), axis=1, keepdims=True))
    return jnp.concatenate(pieces, axis=0)


def z_plan(far, skips):
    plan, held = [], 0
    while held < far:
        hops = 2 if len(plan) < skips and held + 2 <= far else 1
        plan.append([(held, n) for n in range(hops, 0, -1)])
        held += hops
    return plan


def softmax_part(parts):
    scale = HEAD_DIM ** (-0.5) * LOG2E
    top = functools.reduce(
        jnp.maximum, [jnp.max(s, axis=1, keepdims=True) for s, _ in parts]
    )
    total, weighted = 0.0, 0.0
    for s, v in parts:
        exps = jnp.exp2((s - top) * scale)
        total = total + jnp.sum(exps, axis=1, keepdims=True)
        weighted = weighted + jnp.dot(
            exps.astype(jnp.bfloat16), v, preferred_element_type=jnp.float32
        )
    return weighted / total, top * scale + jnp.log(total) * LOG2E


def kernel(
    nx,
    nz,
    ny,
    heads,
    roots,
    z_skips,
    req_len_hbm,
    leaf_mid_hbm,
    mid_root_hbm,
    upper_len_hbm,
    leaf_len_hbm,
    uk,
    uv,
    q_hbm,
    nk_hbm,
    nv_hbm,
    res_hbm,
    w_hbm,
    lk_hbm,
    lv_hbm,
    out,
    *scratch,
):
    kv = scratch[:heads]
    (
        req_len,
        leaf_mid,
        mid_root,
        upper_len,
        leaf_len,
        up,
        qx,
        lk,
        lv,
        nk,
        nv,
        res,
        w,
        leaf_o,
        leaf_lse,
        o_send,
        o_recv,
        s_send,
        s_recv,
        at,
        acc,
        in_sem,
        ring_send,
        ring_recv,
        sib_send,
        sib_recv,
        q_sem,
        w_sem,
        wf_sem,
        o_sem_s,
        o_sem_r,
        s_sem_s,
        s_sem_r,
        y_sem_s,
        y_sem_r,
    ) = scratch[heads:]
    nodes = kv[0].shape[2]
    rows = qx.shape[1]
    width = heads * HEAD_DIM
    half_rows = width // CORES
    tok, y = lax.axis_index("tok"), lax.axis_index("grp")
    c = lax.rem(tok, CORES)
    x = lax.rem(lax.div(tok, CORES), nx)
    z = lax.div(tok, CORES * nx)

    def dev(z_, x_, c_, y_):
        return ((z_ * nx + x_) * CORES + c_, y_)

    sibling = dev(z, x, 1 - c, y)

    def z_mate(hops):
        return dev(lax.rem(z + nz + hops, nz), x, c, y)

    def x_mate(k):
        return lax.rem(x + k, nx)

    def y_mate(k):
        return lax.rem(y + k, ny)

    loads = [
        (uk, up.at[0]),
        (uv, up.at[1]),
        (q_hbm, qx.at[x]),
        (lk_hbm, lk),
        (lv_hbm, lv),
        (nk_hbm, nk),
        (nv_hbm, nv),
        (res_hbm, res),
        (w_hbm.at[:, pl.ds(pl.multiple_of(y * width, width), width)], w.at[y]),
        (req_len_hbm, req_len),
        (leaf_mid_hbm, leaf_mid),
        (mid_root_hbm, mid_root),
        (upper_len_hbm, upper_len),
        (leaf_len_hbm, leaf_len),
    ]
    loads = [pltpu.make_async_copy(a, b, in_sem.at[i]) for i, (a, b) in enumerate(loads)]
    for load in loads:
        load.start()

    partners = [sibling] + [z_mate(hops) for hops in (1, -1, 2, -2)]
    partners += [dev(z, x_mate(k), c, y) for k in range(1, nx)]
    partners += [dev(z, x, c, y_mate(k)) for k in range(1, ny)]
    barrier = pltpu.get_barrier_semaphore()
    for partner in partners:
        pl.semaphore_signal(barrier, inc=1, device_id=partner, device_id_type=MESH)
    loads[0].wait()
    loads[1].wait()
    block = jnp.concatenate(
        [up[i].astype(jnp.float32).reshape(nodes, 8, width) for i in range(2)], axis=1
    ).astype(jnp.bfloat16)
    for h in range(heads):
        kv[h][c, z] = block[:, :, h * HEAD_DIM : (h + 1) * HEAD_DIM]
    pl.semaphore_wait(barrier, len(partners))

    def send(src, dst, send_sem, recv_sem, device):
        pltpu.make_async_remote_copy(
            src_ref=src,
            dst_ref=dst,
            send_sem=send_sem,
            recv_sem=recv_sem,
            device_id=device,
            device_id_type=MESH,
        ).start()

    my_half = pl.ds(pl.multiple_of(c * half_rows, half_rows), half_rows)

    def send_queries():
        for k in sorted(range(1, nx), key=lambda k: -min(k, nx - k)):
            send(q_hbm, qx.at[x], q_sem.at[0], q_sem.at[1], dev(z, x_mate(k), c, y))

    def send_w():
        for k in range(1, ny):
            to = y_mate(k)
            send(
                w_hbm.at[my_half, pl.ds(pl.multiple_of(to * width, width), width)],
                w.at[y, my_half],
                w_sem.at[0],
                w_sem.at[1],
                dev(z, x, c, to),
            )

    far = nz // 2
    cut = nodes // 2

    def z_view(h, direction, distance):
        return kv[h].at[c, lax.rem(z + (nz - distance if direction == 0 else distance), nz)]

    def z_part(h, direction, held, distance):
        view = z_view(h, direction, held)
        if distance == far:
            view = view.at[pl.ds(0, cut)] if direction == 0 else view.at[pl.ds(cut, nodes - cut)]
        return view

    def z_wait(h, direction, distance):
        wait_bytes(
            z_part(h, direction, distance, distance), ring_recv.at[h, direction, distance - 1]
        )

    def share(h, view):
        send(view, view, sib_send.at[h], sib_recv.at[h], sibling)

    plans = [z_plan(far, z_skips[min(h, len(z_skips) - 1)]) for h in range(heads)]

    def z_stage(h, stage):
        came = [0] if stage == 0 else [held + hops for held, hops in plans[h][stage - 1]]
        go_on = sorted({held for held, _ in plans[h][stage]}) if stage < len(plans[h]) else []
        for held in go_on:
            if held:
                for direction in range(2):
                    z_wait(h, direction, held)
        for held, hops in plans[h][stage] if stage < len(plans[h]) else ():
            for direction in range(2):
                view = z_part(h, direction, held, held + hops)
                send(
                    view,
                    view,
                    ring_send.at[h],
                    ring_recv.at[h, direction, held + hops - 1],
                    z_mate(hops if direction == 0 else -hops),
                )
        for distance in sorted(came, key=lambda d: d not in go_on):
            if distance == 0:
                share(h, kv[h].at[c, z])
                continue
            for direction in range(2):
                if distance not in go_on:
                    z_wait(h, direction, distance)
                if distance < far:
                    share(h, z_view(h, direction, distance))
            if distance == far:
                share(h, z_view(h, 0, far))

    me = tok
    position = lax.broadcasted_iota(jnp.int32, (rows, 1), 0)

    def leaf_part(h):
        cols = slice(h * HEAD_DIM, (h + 1) * HEAD_DIM)
        query = qx[x, :, cols]
        leaf_scores = dot_nt(query, lk[:, cols])
        at_pos = lax.broadcasted_iota(jnp.int32, leaf_scores.shape, 1)
        leaf_scores = jnp.where(at_pos < leaf_len[me], leaf_scores, NEG_FILL)
        new_scores = dot_nt(query, nk[:, cols])
        key_pos = lax.broadcasted_iota(jnp.int32, new_scores.shape, 1)
        query_pos = lax.broadcasted_iota(jnp.int32, new_scores.shape, 0)
        allowed = (key_pos <= query_pos) & (key_pos < req_len[me])
        new_scores = jnp.where(allowed, new_scores, NEG_FILL)
        o, lse = softmax_part([(leaf_scores, lv[:, cols]), (new_scores, nv[:, cols])])
        leaf_o[h] = o
        leaf_lse[h] = jnp.broadcast_to(lse, (rows, HEAD_DIM))

    def leaf_head(h):
        if h == 0:
            for load in loads[2:7] + loads[9:]:
                load.wait()
        leaf_part(h)

    def share_w():
        wait_bytes(w.at[pl.ds(0, ny - 1), pl.ds(0, half_rows)], w_sem.at[1])
        for k in range(1, ny):
            view = w.at[y_mate(k), my_half]
            send(view, view, wf_sem.at[0], wf_sem.at[1], sibling)

    keys = nz * 16

    def upper_part(h, j):
        request = (z * nx + j) * CORES + c
        mid = leaf_mid[request]
        root = mid_root[mid]
        query = qx[j, :, h * HEAD_DIM : (h + 1) * HEAD_DIM]

        def rows_of(node):
            both = kv[h][:, :, node].astype(jnp.float32).reshape(keys // 8, 16, HEAD_DIM)
            return (
                both[:, :8].reshape(keys, HEAD_DIM).astype(jnp.bfloat16),
                both[:, 8:].reshape(keys, HEAD_DIM).astype(jnp.bfloat16),
            )

        root_keys, root_values = rows_of(root)
        mid_keys, mid_values = rows_of(roots + mid)
        root_scores = dot_nt(query, root_keys)
        mid_scores = dot_nt(query, mid_keys)
        key = lax.broadcasted_iota(jnp.int32, mid_scores.shape, 1)
        core = (key >= keys // 2).astype(jnp.int32)
        key = key - core * (keys // 2)
        key_pos = (key >> 3) * (nx * 16) + x * 16 + core * 8 + (key & 7)
        root_scores = jnp.where(key_pos < upper_len[root], root_scores, NEG_FILL)
        mid_scores = jnp.where(key_pos < upper_len[roots + mid], mid_scores, NEG_FILL)
        o, lse = softmax_part([(root_scores, root_values), (mid_scores, mid_values)])
        row = col_to_row(lse)
        return o.astype(jnp.bfloat16), jnp.broadcast_to(row, (8, row.shape[1]))

    def upper_head(h):
        if h == 0:
            wait_bytes(qx.at[pl.ds(0, nx - 1)], q_sem.at[1])
        wait_bytes(kv[h].at[1 - c], sib_recv.at[h])

        @pl.loop(0, nx - 1)
        def _(k):
            j = lax.rem(x + lax.rem(k + nx // 2 - 1, nx - 1) + 1, nx)
            o, lse = upper_part(h, j)
            o_send[h, j] = o
            s_send[h, j] = lse
            to = dev(z, j, c, y)
            send(s_send.at[h, j], s_recv.at[h, x], s_sem_s.at[h], s_sem_r.at[h], to)
            send(o_send.at[h, j], o_recv.at[h, x], o_sem_s.at[h], o_sem_r.at[h], to)

        o, lse = upper_part(h, x)
        o_recv[h, x] = o
        s_recv[h, x] = lse

    def merge_head(h):
        wait_bytes(s_recv.at[h, pl.ds(0, nx - 1)], s_sem_r.at[h])
        wait_bytes(o_recv.at[h, pl.ds(0, nx - 1)], o_sem_r.at[h])
        sums = [row_to_col(s_recv[h, i, 0:1, :], rows) for i in range(nx)]
        sums.append(leaf_lse[h][:, 0:1])
        top = functools.reduce(jnp.maximum, sums)
        total, weighted = 0.0, 0.0
        for i in range(nx + 1):
            weight = jnp.exp2(sums[i] - top)
            part = o_recv[h, i].astype(jnp.float32) if i < nx else leaf_o[h]
            total = total + weight
            weighted = weighted + weight * part
        attended = jnp.where(position < req_len[me], weighted / total, 0.0)
        at[h, y] = attended.astype(jnp.bfloat16)
        for k in sorted(range(1, ny), key=lambda k: -min(k, ny - k)):
            view = at.at[h, y]
            send(view, view, y_sem_s.at[h], y_sem_r.at[h], dev(z, x, c, y_mate(k)))

    def project_head(h):
        if h == 0:
            loads[8].wait()
            wait_bytes(w.at[pl.ds(0, ny - 1), pl.ds(0, half_rows)], wf_sem.at[1])
        wait_bytes(at.at[h, pl.ds(0, ny - 1)], y_sem_r.at[h])
        total = res[...].astype(jnp.float32) if h == 0 else acc[...]
        for i in range(ny):
            total = total + jnp.dot(
                at[h, i],
                w[i, h * HEAD_DIM : (h + 1) * HEAD_DIM, :],
                preferred_element_type=jnp.float32,
            )
        if h < heads - 1:
            acc[...] = total
        else:
            out[...] = total.astype(out.dtype)

    events = [(Q_AT, send_queries), (W_FROM, send_w), (W_AT, share_w)]
    for h in range(heads):
        for stage in range(len(plans[h]) + 1):
            events.append((stage + OFFSETS[h], functools.partial(z_stage, h, stage)))
        end = len(plans[h]) + OFFSETS[h]
        events.append((LEAF_AT[h], functools.partial(leaf_head, h)))
        events.append((end + UPPER_AT, functools.partial(upper_head, h)))
        events.append((end + MERGE_AT, functools.partial(merge_head, h)))
        events.append((end + PROJECT_AT, functools.partial(project_head, h)))
    loads[7].wait()
    for _, event in sorted(events, key=lambda item: item[0]):
        event()

    wait_bytes(qx.at[pl.ds(0, nx - 1)], q_sem.at[0])
    wait_bytes(w.at[pl.ds(0, ny - 1), pl.ds(0, half_rows)], w_sem.at[0])
    wait_bytes(w.at[pl.ds(0, ny - 1), pl.ds(0, half_rows)], wf_sem.at[0])
    for h in range(heads):
        wait_bytes(kv[h].at[0, pl.ds(0, nz - 1)], ring_send.at[h])
        wait_bytes(kv[h].at[0], sib_send.at[h])
        wait_bytes(s_recv.at[h, pl.ds(0, nx - 1)], s_sem_s.at[h])
        wait_bytes(o_recv.at[h, pl.ds(0, nx - 1)], o_sem_s.at[h])
        wait_bytes(at.at[h, pl.ds(0, ny - 1)], y_sem_s.at[h])


def shards(
    nx,
    queries,
    new_keys,
    new_values,
    residual,
    w_out,
    leaf_keys,
    leaf_values,
    upper_keys,
    upper_values,
    req_len,
    leaf_mid,
    mid_root,
    upper_len,
    leaf_len,
):
    ny = lax.axis_size("grp")
    nz = lax.axis_size("tok") // (nx * CORES)
    rows, width = queries.shape
    heads = width // HEAD_DIM
    nodes, depth, _ = upper_keys.shape
    leaf_pos = leaf_keys.shape[1]
    roots = nodes - mid_root.shape[0]
    stat_width = -(-rows // 128) * 128
    bf16, f32 = jnp.bfloat16, jnp.float32
    dma = pltpu.SemaphoreType.DMA
    scratch = [pltpu.VMEM((2, nz, nodes, 16, HEAD_DIM), bf16) for _ in range(heads)]
    scratch += [pltpu.SMEM(a.shape, a.dtype) for a in (req_len, leaf_mid, mid_root, upper_len, leaf_len)]
    scratch += [
        pltpu.VMEM((2, nodes * depth, width), bf16),
        pltpu.VMEM((nx, rows, width), bf16),
        pltpu.VMEM((leaf_pos, width), bf16),
        pltpu.VMEM((leaf_pos, width), bf16),
        pltpu.VMEM((rows, width), bf16),
        pltpu.VMEM((rows, width), bf16),
        pltpu.VMEM((rows, width), bf16),
        pltpu.VMEM((ny, width, width), bf16),
        pltpu.VMEM((heads, rows, HEAD_DIM), f32),
        pltpu.VMEM((heads, rows, HEAD_DIM), f32),
        pltpu.VMEM((heads, nx, rows, HEAD_DIM), bf16),
        pltpu.VMEM((heads, nx, rows, HEAD_DIM), bf16),
        pltpu.VMEM((heads, nx, 8, stat_width), f32),
        pltpu.VMEM((heads, nx, 8, stat_width), f32),
        pltpu.VMEM((heads, ny, rows, HEAD_DIM), bf16),
        pltpu.VMEM((rows, width), f32),
        dma((14,)),
        dma((heads,)),
        dma((heads, 2, nz // 2)),
        dma((heads,)),
        dma((heads,)),
        dma((2,)),
        dma((2,)),
        dma((2,)),
        dma((heads,)),
        dma((heads,)),
        dma((heads,)),
        dma((heads,)),
        dma((heads,)),
        dma((heads,)),
    ]
    hbm = pl.BlockSpec(memory_space=pltpu.HBM)
    return pl.pallas_call(
        functools.partial(kernel, nx, nz, ny, heads, roots, Z_SKIPS),
        out_shape=jax.ShapeDtypeStruct((rows, width), bf16),
        in_specs=[hbm] * 14,
        out_specs=pl.BlockSpec(memory_space=pltpu.VMEM),
        scratch_shapes=scratch,
        compiler_params=pltpu.CompilerParams(
            collective_id=0, has_side_effects=True, vmem_limit_bytes=63 * 1024 * 1024
        ),
    )(
        req_len,
        leaf_mid,
        mid_root,
        upper_len,
        leaf_len,
        upper_keys.reshape(nodes * depth, width),
        upper_values.reshape(nodes * depth, width),
        queries,
        new_keys,
        new_values,
        residual,
        w_out,
        leaf_keys.reshape(leaf_pos, width),
        leaf_values.reshape(leaf_pos, width),
    )


def solution(mesh, nx=CHIPS_X):
    in_specs = (
        P("tok", "grp"),
        P("tok", "grp"),
        P("tok", "grp"),
        P("tok", "grp"),
        P("grp", None),
        P("tok", None, "grp"),
        P("tok", None, "grp"),
        P(None, "tok", "grp"),
        P(None, "tok", "grp"),
        P(),
        P(),
        P(),
        P(),
        P(),
    )
    return jax.shard_map(
        functools.partial(shards, nx),
        mesh=mesh,
        in_specs=in_specs,
        out_specs=P("tok", "grp"),
        check_vma=False,
    )
```
